256 devices in a mesh: pipe: 8 (over y_lo, x), fsdp: 32 (over z, y_hi, core).
Axes of the slice: x: 4, y: 4 (y_hi: 2, y_lo: 2; y = y_hi * 2 + y_lo), z: 8, core: 2. Of those that a mesh axis runs over, the one named last changes fastest.
Arguments:
- tokens: bfloat16 [512, 12288], P(None, 'pipe'), may hold values from -6 to 6
- cotangent: bfloat16 [512, 12288], P(None, 'pipe'), may hold values from -6 to 6
- gate_weight: bfloat16 [12288, 28672], P('pipe', 'fsdp'), may hold values from -0.0546875 to 0.0546875
- up_weight: bfloat16 [12288, 28672], P('pipe', 'fsdp'), may hold values from -0.0546875 to 0.0546875
- down_weight: bfloat16 [28672, 12288], P('fsdp', 'pipe'), may hold values from -0.0546875 to 0.0546875
- adapter_down_first: bfloat16 [28672, 64], P('fsdp'), may hold values from -0.03125 to 0.03125
- adapter_down_second: bfloat16 [64, 12288], P(None, 'pipe'), may hold values from -0.29882812 to 0.29882812
Outputs:
- grad_input: bfloat16 [512, 12288], P('fsdp', 'pipe')
- grad_lora_a: float32 [28672, 64], P('fsdp')
- grad_lora_b: float32 [64, 12288], P(None, 'pipe')
The draws below stay inside these ranges and needn't reach their ends.
All inputs are finite; a program needn't handle non-finite values.
Results may differ from the reference program's by a relative error of at most 0.005.
Values may be sent and summed in bfloat16 or wider, within the bound.
A program may use at most 64 MiB of HBM per device.

```python
import jax
import jax.numpy as jnp

MODEL_WIDTH = 12288
HIDDEN_UNITS = 28672
ADAPTER_RANK = 64
TOKENS = 512


def block_levels(stream_key, dims, cuts, least, top_value):
    gain = 1.0
    for dim, parts in cuts:
        steps = jax.random.uniform(jax.random.fold_in(jax.random.fold_in(stream_key, 6), dim), (parts,), jnp.float32, least / len(cuts), top_value / len(cuts))
        gain = gain * jnp.repeat(jnp.exp(steps), dims[dim] // parts).reshape((-1,) + (1,) * (len(dims) - 1 - dim))
    return gain


def normal_values(rng, dims, deviation, limit, split=(), dtype=jnp.bfloat16):
    entries = deviation * jax.random.normal(rng, dims, jnp.float32)
    if split:
        entries = entries * block_levels(rng, dims, split, -0.22, 0.18)
    return jnp.clip(entries, -limit, limit).astype(dtype)


def setup_inputs(seed: int = 0) -> dict:
    arg_keys = jax.random.split(jax.random.key(seed), 8)
    tokens = normal_values(arg_keys[0], (TOKENS, MODEL_WIDTH), 1.0, 6.0, ((1, 8),))
    cotangent = normal_values(arg_keys[1], (TOKENS, MODEL_WIDTH), 1.0, 6.0, ((1, 8),))
    gate_weight = normal_values(arg_keys[2], (MODEL_WIDTH, HIDDEN_UNITS), MODEL_WIDTH ** -0.5, 0.0546875, ((0, 8), (1, 32)))
    up_weight = normal_values(arg_keys[3], (MODEL_WIDTH, HIDDEN_UNITS), MODEL_WIDTH ** -0.5, 0.0546875, ((0, 8), (1, 32)))
    down_weight = normal_values(arg_keys[4], (HIDDEN_UNITS, MODEL_WIDTH), MODEL_WIDTH ** -0.5, 0.0546875, ((0, 32), (1, 8)))
    adapter_down_first = normal_values(arg_keys[5], (HIDDEN_UNITS, ADAPTER_RANK), HIDDEN_UNITS ** -0.5, 0.03125, ((0, 32),))
    adapter_down_second = normal_values(arg_keys[6], (ADAPTER_RANK, MODEL_WIDTH), 0.05, 0.29882812, ((1, 8),))
    return {"tokens": tokens, "cotangent": cotangent, "gate_weight": gate_weight, "up_weight": up_weight, "down_weight": down_weight, "adapter_down_first": adapter_down_first, "adapter_down_second": adapter_down_second}


adapter_scale = 0.5


def reference(tokens, cotangent, gate_weight, up_weight, down_weight, adapter_down_first, adapter_down_second):
    gate = jnp.dot(tokens, gate_weight, preferred_element_type=jnp.float32)
    up_values = jnp.dot(tokens, up_weight, preferred_element_type=jnp.float32)
    sigmoid_gate = jax.nn.sigmoid(gate)
    silu_gate = gate * sigmoid_gate
    hidden_activation = (silu_gate * up_values).astype(jnp.bfloat16)
    lowrank_product = jnp.dot(hidden_activation, adapter_down_first, preferred_element_type=jnp.float32).astype(jnp.bfloat16)
    backward_lowrank = jnp.dot(cotangent, adapter_down_second.T, preferred_element_type=jnp.float32).astype(jnp.bfloat16)
    hidden_gradient = jnp.dot(cotangent, down_weight.T, preferred_element_type=jnp.float32)
    hidden_gradient = hidden_gradient + adapter_scale * jnp.dot(backward_lowrank, adapter_down_first.T, preferred_element_type=jnp.float32)
    grad_gate = (hidden_gradient * up_values * sigmoid_gate * (1.0 + gate * (1.0 - sigmoid_gate))).astype(jnp.bfloat16)
    grad_up = (hidden_gradient * silu_gate).astype(jnp.bfloat16)
    grad_input = jnp.dot(grad_gate, gate_weight.T, preferred_element_type=jnp.float32)
    grad_input = (grad_input + jnp.dot(grad_up, up_weight.T, preferred_element_type=jnp.float32)).astype(jnp.bfloat16)
    gradient_factor_first = adapter_scale * jnp.dot(hidden_activation.T, backward_lowrank, preferred_element_type=jnp.float32)
    gradient_factor_second = adapter_scale * jnp.dot(lowrank_product.T, cotangent, preferred_element_type=jnp.float32)
    return grad_input, gradient_factor_first, gradient_factor_second
```

```python
import jax
import jax.numpy as jnp
from jax import lax
from jax.experimental import pallas as pl
from jax.experimental.pallas import tpu as pltpu
from jax.sharding import PartitionSpec as P

F32 = jnp.float32
BF16 = jnp.bfloat16
MESH = pl.DeviceIdType.MESH

TOK = 512
FEAT = 1536
HID = 896
RANK = 64
BATCHES = 4
ROWS = 128
BLK = 16
XW = 512
YW = 384
SPLIT = (0, 640, 1152)
N_COPIES = 200
N_LOADS = 20


def dot(a, b):
    return jnp.dot(a, b, preferred_element_type=F32)


def dot_t(a, b):
    return lax.dot_general(a, b, (((1,), (1,)), ((), ())), preferred_element_type=F32)


def dot_lead(a, b):
    return lax.dot_general(a, b, (((0,), (0,)), ((), ())), preferred_element_type=F32)


def pack(v):
    return jnp.concatenate([v[:32], v[32:]], axis=1)


def unpack(v):
    return jnp.concatenate([v[:, :64], v[:, 64:]], axis=0)


class Bag:
    pass


class Copies:
    def __getattr__(self, name):
        made = {}
        setattr(self, name, made)
        return made


def scratch_spec():
    specs = []
    v = Bag()

    def new(shape, dtype):
        specs.append(pltpu.VMEM(shape, dtype))
        return len(specs) - 1

    n = BATCHES
    v.tok = new((n, 8, BLK, FEAT), BF16)
    v.cot = new((n, 8, BLK, FEAT), BF16)
    v.gw = new((FEAT, HID), BF16)
    v.uw = new((FEAT, HID), BF16)
    v.dw = new((HID, FEAT), BF16)
    v.down_a = new((RANK, HID), BF16)
    v.down_b = new((RANK, FEAT), BF16)
    wide = 3 * XW
    v.xpart = new((n, ROWS, wide), F32)
    v.xfd_s = new((n, 4, BLK, wide), BF16)
    v.xfd_r = new((n, 4, BLK, wide), BF16)
    v.xc_s = new((n, 2, BLK, wide), BF16)
    v.xc_r = new((n, 2, BLK, wide), BF16)
    v.xsum = new((n, 2, BLK, wide), F32)
    v.xy_s = new((n, BLK, wide), BF16)
    v.xy_r = new((n, BLK, wide), BF16)
    v.xgrad = new((n, ROWS, 2 * XW), BF16)
    wide = 3 * YW
    v.ypart = new((n, ROWS, wide), F32)
    v.yy_s = new((n, 64, wide), BF16)
    v.yy_r = new((n, 64, wide), BF16)
    v.ysum = new((n, 64, wide), F32)
    v.yfd_s = new((n, 2, BLK, wide), BF16)
    v.yfd_r = new((n, 2, BLK, wide), BF16)
    v.yc_s = new((n, BLK, wide), BF16)
    v.yc_r = new((n, BLK, wide), BF16)
    v.ygrad = new((n, ROWS, 2 * YW), BF16)
    v.hidden = new((TOK // 8, HID), BF16)
    v.acc = new((n, ROWS, FEAT), F32)
    v.back = new((n, 8, BLK, RANK), F32)
    v.back_s = new((8, 32, 128), BF16)
    v.back_r = new((8, 32, 128), BF16)
    v.la_s = new((RANK, HID), F32)
    v.la_r = new((8, 8, HID), F32)
    v.la = new((RANK, HID), F32)
    v.low_s = new((32, 128), F32)
    v.low_cr = new((32, 128), F32)
    v.low_h = new((16, 128), F32)
    v.low_zr = new((16, 16, 128), F32)
    v.low_p = new((2, 8, 16, 128), BF16)
    v.core_r = new((n, ROWS, FEAT), F32)
    v.z_s = new((n, 8, BLK, FEAT), BF16)
    v.z_r = new((n, 8, BLK, FEAT), BF16)
    v.yh_s = new((n, BLK, FEAT), F32)
    v.yh_r = new((n, BLK, FEAT), F32)
    return specs, v


def kernel(*refs):
    specs, places = scratch_spec()
    tok_h, cot_h, gw_h, uw_h, dw_h, a_h, b_h, gi_o, la_o, lb_o = refs[:10]
    held = refs[10 : 10 + len(specs)]
    send_sems, recv_sems, load_sems = refs[10 + len(specs) :]
    S = Bag()
    for name, place in vars(places).items():
        setattr(S, name, held[place])

    p = lax.axis_index("pipe")
    f = lax.axis_index("fsdp")
    x = lax.rem(p, 4)
    y = lax.div(p, 4)
    z = lax.div(f, 4)
    yh = lax.rem(lax.div(f, 2), 2)
    core = lax.rem(f, 2)
    chip = lax.div(f, 2)
    x_p, x_m, x_f = lax.rem(x + 1, 4), lax.rem(x + 3, 4), lax.rem(x + 2, 4)

    def pipe(i):
        return {"pipe": i}

    def fsdp(i):
        return {"fsdp": i}

    to_xp = pipe(y * 4 + x_p)
    to_xm = pipe(y * 4 + x_m)
    to_y = pipe((1 - y) * 4 + x)
    to_core = fsdp(f + 1 - 2 * core)
    to_yh = fsdp(f + 2 - 4 * yh)

    count = [0]
    sent = []

    def remote(src, dst, dev):
        i = count[0]
        count[0] += 1
        return pltpu.make_async_remote_copy(
            src_ref=src,
            dst_ref=dst,
            send_sem=send_sems.at[i],
            recv_sem=recv_sems.at[i],
            device_id=dev,
            device_id_type=MESH,
        )

    def go(cp, cond=None):
        cp.start()
        sent.append((cp, cond))
        return cp

    loads = {}

    def load(key, dst, src):
        cp = pltpu.make_async_copy(src, dst, load_sems.at[len(loads)])
        cp.start()
        loads[key] = cp

    XC, YC = slice(0, XW), slice(XW, HID)
    xcols, ycols = pl.ds(0, XW), pl.ds(XW, YW)
    TOKENS, COT, GATE_W, UP_W, DOWN_W, DOWN_A, DOWN_B = range(7)
    load((TOKENS, 0), S.tok.at[0], tok_h.at[:, 0])
    load((GATE_W, 0), S.gw.at[:, xcols], gw_h.at[:, xcols])
    load((UP_W, 0), S.uw.at[:, xcols], uw_h.at[:, xcols])
    load((COT, 0), S.cot.at[0], cot_h.at[:, 0])
    load(DOWN_B, S.down_b, b_h)
    load(DOWN_A, S.down_a, a_h)
    load((DOWN_W, 0), S.dw.at[xcols], dw_h.at[xcols])
    load((GATE_W, 1), S.gw.at[:, ycols], gw_h.at[:, ycols])
    load((UP_W, 1), S.uw.at[:, ycols], uw_h.at[:, ycols])
    load((DOWN_W, 1), S.dw.at[ycols], dw_h.at[ycols])
    for i in range(1, BATCHES):
        load((TOKENS, i), S.tok.at[i], tok_h.at[:, i])
        load((COT, i), S.cot.at[i], cot_h.at[:, i])

    barrier = pltpu.get_barrier_semaphore()
    peers = [pipe(lax.rem(p + j, 8)) for j in range(1, 8)]
    peers += [to_core]
    peers += [fsdp(lax.rem(chip + j, 16) * 2 + core) for j in range(1, 16)]
    for dev in peers:
        pl.semaphore_signal(barrier, inc=1, device_id=dev, device_id_type=MESH)

    def block(x_, y_):
        return pl.ds(pl.multiple_of((y_ * 4 + x_) * BLK, BLK), BLK)

    def quarter(x_):
        return pl.ds(pl.multiple_of(x_ * BLK, BLK), BLK)

    def half(y_):
        return pl.ds(pl.multiple_of(y_ * 64, 64), 64)

    def side(k):
        return slice(SPLIT[k], SPLIT[k + 1])

    def side_d(k):
        return pl.ds(SPLIT[k], SPLIT[k + 1] - SPLIT[k])

    st = Copies()

    def whole(ref, i):
        return ref[i].reshape(ROWS, FEAT)

    def products(i, part, cols, w):
        tok, cot = whole(S.tok, i), whole(S.cot, i)
        part[i, :, 0:w] = dot(tok, S.gw[:, cols])
        part[i, :, w : 2 * w] = dot(tok, S.uw[:, cols])
        back = (0.5 * S.back[i].reshape(ROWS, RANK)).astype(BF16)
        part[i, :, 2 * w :] = dot_t(cot, S.dw[cols, :]) + dot(back, S.down_a[:, cols])

    def a1(i):
        if i == 0:
            for key in ((TOKENS, 0), (COT, 0), DOWN_A, DOWN_B):
                loads[key].wait()
            for kind in (GATE_W, UP_W, DOWN_W):
                loads[kind, 0].wait()
        else:
            loads[TOKENS, i].wait()
            loads[COT, i].wait()
        S.back[i] = dot_t(whole(S.cot, i), S.down_b[...]).reshape(8, BLK, RANK)
        products(i, S.xpart, XC, XW)
        if i == 0:
            pl.semaphore_wait(barrier, len(peers))
        plan = ((x_f, 0, to_xp), (x_f, 1, to_xm), (x_p, 1, to_xp), (x_m, 0, to_xm))
        for k, (bx, by, dev) in enumerate(plan):
            S.xfd_s[i, k] = S.xpart[i, block(bx, by), :].astype(BF16)
            st.xfd[i, k] = go(remote(S.xfd_s.at[i, k], S.xfd_r.at[i, k], dev))
        if i == 0:
            for kind in (GATE_W, UP_W, DOWN_W):
                loads[kind, 1].wait()
        products(i, S.ypart, YC, YW)
        S.yy_s[i] = S.ypart[i, half(1 - y), :].astype(BF16)
        st.yy[i] = go(remote(S.yy_s.at[i], S.yy_r.at[i], to_y))

    def a2(i):
        for k, rows, dev in ((0, block(x_p, 0), to_xp), (1, block(x_m, 1), to_xm)):
            st.xfd[i, k].wait_recv()
            S.xc_s[i, k] = (S.xpart[i, rows, :] + S.xfd_r[i, k].astype(F32)).astype(BF16)
            st.xc[i, k] = go(remote(S.xc_s.at[i, k], S.xc_r.at[i, k], dev))
        st.yy[i].wait_recv()
        S.ysum[i] = S.ypart[i, half(y), :] + S.yy_r[i].astype(F32)
        plan = ((0, 0, x_f, to_xp), (0, 1, x_f, to_xm), (1, 1, x_p, to_xp), (1, 0, x_m, to_xm))
        for k, s, bx, dev in plan:
            S.yfd_s[i, k, :, side(s)] = S.ysum[i, quarter(bx), side(s)].astype(BF16)
            st.yfd[i, k, s] = go(
                remote(
                    S.yfd_s.at[i, k, :, side_d(s)], S.yfd_r.at[i, k, :, side_d(s)], dev
                )
            )

    def a3(i):
        for k in (2, 3):
            st.xfd[i, k].wait_recv()
        for k in (0, 1):
            st.xc[i, k].wait_recv()
        for k in (0, 1):
            S.xsum[i, k] = (
                S.xpart[i, block(x, k), :]
                + S.xfd_r[i, 3 - k].astype(F32)
                + S.xc_r[i, k].astype(F32)
            )
        S.xy_s[i] = S.xsum[i, 1 - y].astype(BF16)
        st.xy[i] = go(remote(S.xy_s.at[i], S.xy_r.at[i], to_y))
        for s, bx, dev in ((0, x_p, to_xp), (1, x_m, to_xm)):
            st.yfd[i, 0, s].wait_recv()
            S.yc_s[i, :, side(s)] = (
                S.ysum[i, quarter(bx), side(s)] + S.yfd_r[i, 0, :, side(s)].astype(F32)
            ).astype(BF16)
            st.yc[i, s] = go(
                remote(S.yc_s.at[i, :, side_d(s)], S.yc_r.at[i, :, side_d(s)], dev)
            )

    def activate(i, total, w, grad, cols):
        gate, up, hg = total[:, :w], total[:, w : 2 * w], total[:, 2 * w :]
        sig = jax.nn.sigmoid(gate)
        silu = gate * sig
        mine = block(x, y)
        grad[i, mine, 0:w] = (hg * up * sig * (1.0 + gate * (1.0 - sig))).astype(BF16)
        grad[i, mine, w : 2 * w] = (hg * silu).astype(BF16)
        S.hidden[i * BLK : (i + 1) * BLK, cols] = (silu * up).astype(BF16)

    def a4(i):
        st.xy[i].wait_recv()
        activate(i, S.xsum[i, y] + S.xy_r[i].astype(F32), XW, S.xgrad, XC)
        slot = S.xgrad.at[i, block(x, y)]
        st.xown_y[i] = go(remote(slot, slot, to_y))
        st.xown_p[i] = go(remote(slot, slot, to_xp))
        st.xown_m[i] = go(remote(slot, slot, to_xm))
        for s in (0, 1):
            st.yfd[i, 1, s].wait_recv()
            st.yc[i, s].wait_recv()
        total = (
            S.ysum[i, quarter(x), :] + S.yfd_r[i, 1].astype(F32) + S.yc_r[i].astype(F32)
        )
        activate(i, total, YW, S.ygrad, YC)
        slot = S.ygrad.at[i, block(x, y)]
        st.yown_p[i] = go(remote(slot, slot, to_xp))
        st.yown_m[i] = go(remote(slot, slot, to_xm))
        st.yown_y[i] = go(remote(slot, slot, to_y))

    def b2(i):
        st.xown_y[i].wait_recv()
        slot = S.xgrad.at[i, block(x, 1 - y)]
        st.xoth_p[i] = go(remote(slot, slot, to_xp))
        st.xoth_m[i] = go(remote(slot, slot, to_xm))
        left, right = pl.ds(0, YW), pl.ds(YW, YW)
        st.yown_p[i].wait_recv()
        part = S.ygrad.at[i, block(x_m, y), left]
        st.yfar_p[i] = go(remote(part, part, to_xp))
        slot = S.ygrad.at[i, block(x_m, y)]
        st.yy_m[i] = go(remote(slot, slot, to_y))
        st.yown_m[i].wait_recv()
        part = S.ygrad.at[i, block(x_p, y), right]
        st.yfar_m[i] = go(remote(part, part, to_xm))
        slot = S.ygrad.at[i, block(x_p, y)]
        st.yy_p[i] = go(remote(slot, slot, to_y))

    def b3(i):
        st.xown_p[i].wait_recv()
        slot = S.xgrad.at[i, block(x_m, y)]
        st.xfar_p[i] = go(remote(slot, slot, to_xp))
        st.xoth_m[i].wait_recv()
        slot = S.xgrad.at[i, block(x_p, 1 - y)]
        st.xfar_m[i] = go(remote(slot, slot, to_xm))
        st.yfar_p[i].wait_recv()
        st.yfar_m[i].wait_recv()
        slot = S.ygrad.at[i, block(x_f, y)]
        st.yy_f[i] = go(remote(slot, slot, to_y))

    def owner_core(i):
        return i % 2

    def owner_yh(i):
        return i // 2

    def b4(i):
        for copies in (st.xown_m, st.xoth_p, st.xfar_p, st.xfar_m):
            copies[i].wait_recv()
        v = dot_t(S.xgrad[i, :, 0:XW], S.gw[:, XC]) + dot_t(S.xgrad[i, :, XW:], S.uw[:, XC])
        S.acc[i] = v
        for copies in (st.yown_y, st.yy_m, st.yy_p, st.yy_f):
            copies[i].wait_recv()
        v = dot_t(S.ygrad[i, :, 0:YW], S.gw[:, YC]) + dot_t(S.ygrad[i, :, YW:], S.uw[:, YC])
        S.acc[i] += v
        st.core[i] = remote(S.acc.at[i], S.core_r.at[i], to_core)
        away = core != owner_core(i)

        @pl.when(away)
        def _():
            go(st.core[i], away)

    def z_rows(j):
        return pl.ds(pl.multiple_of(lax.rem(z + j, 8) * BLK, BLK), BLK)

    def c2(i):
        here = core == owner_core(i)
        for j in range(1, 8):
            dev = fsdp(lax.rem(f + 4 * j, 32))
            st.z[i, j] = remote(S.z_s.at[i, j], S.z_r.at[i, j], dev)

        @pl.when(here)
        def _():
            st.core[i].wait_recv()
            for j in (4, 3, 5, 2, 6, 1, 7):
                rows = z_rows(j)
                S.z_s[i, j] = (S.acc[i, rows, :] + S.core_r[i, rows, :]).astype(BF16)
                go(st.z[i, j], here)

    def c3(i):
        here = core == owner_core(i)
        away = jnp.logical_and(here, yh != owner_yh(i))
        st.yh[i] = remote(S.yh_s.at[i], S.yh_r.at[i], to_yh)

        @pl.when(here)
        def _():
            rows = z_rows(0)
            total = S.acc[i, rows, :] + S.core_r[i, rows, :]
            for j in (1, 7, 2, 6, 3, 5, 4):
                st.z[i, j].wait_recv()
                total = total + S.z_r[i, j].astype(F32)
            S.yh_s[i] = total

        @pl.when(away)
        def _():
            go(st.yh[i], away)

    def c4(i):
        @pl.when(jnp.logical_and(core == owner_core(i), yh == owner_yh(i)))
        def _():
            st.yh[i].wait_recv()
            gi_o[...] = (S.yh_s[i] + S.yh_r[i]).astype(BF16)

    def back_send():
        for b in range(8):
            rows = jnp.concatenate([S.back[i, b] for i in range(BATCHES)], axis=0)
            S.back_s[b] = pack(rows).astype(BF16)
        for j in range(1, 8):
            dst = lax.rem(p + j, 8)
            st.back[j] = go(remote(S.back_s.at[dst], S.back_r.at[j], pipe(dst)))

    def low_1():
        S.low_s[...] = pack(dot_t(S.hidden[...], S.down_a[...]))
        st.low_c[0] = go(remote(S.low_s, S.low_cr, to_core))
        total = S.back_s[p].astype(F32)
        for j in range(1, 8):
            st.back[j].wait_recv()
            total = total + S.back_r[j].astype(F32)
        back = (0.5 * unpack(total)).astype(BF16)
        S.la_s[...] = dot_lead(back, S.hidden[...])
        for j in range(1, 8):
            dst = lax.rem(p + j, 8)
            rows = S.la_s.at[pl.ds(pl.multiple_of(dst * 8, 8), 8)]
            st.la[j] = go(remote(rows, S.la_r.at[j], pipe(dst)))

    def low_2():
        st.low_c[0].wait_recv()
        rows = pl.ds(pl.multiple_of(core * 16, 16), 16)
        S.low_h[...] = S.low_s[rows, :] + S.low_cr[rows, :]
        for j in range(1, 16):
            dev = fsdp(lax.rem(chip + j, 16) * 2 + core)
            st.low_z[j] = go(remote(S.low_h, S.low_zr.at[j], dev))

    def la_2():
        mine = pl.ds(pl.multiple_of(p * 8, 8), 8)
        total = S.la_s[mine, :]
        for j in range(1, 8):
            st.la[j].wait_recv()
            total = total + S.la_r[j]
        S.la[mine, :] = total
        slot = S.la.at[mine]
        for j in range(1, 8):
            st.la_g[j] = go(remote(slot, slot, pipe(lax.rem(p + j, 8))))

    def low_3():
        total = S.low_h[...]
        for j in range(1, 16):
            st.low_z[j].wait_recv()
            total = total + S.low_zr[j]
        S.low_p[core, p] = total.astype(BF16)
        slot = S.low_p.at[core, p]
        for j in range(1, 8):
            st.low_p[j] = go(remote(slot, slot, pipe(lax.rem(p + j, 8))))

    def low_4():
        for j in range(1, 8):
            st.low_p[j].wait_recv()
        slot = S.low_p.at[core]
        st.low_g[0] = go(remote(slot, slot, to_core))

    def la_3():
        for j in range(1, 8):
            st.la_g[j].wait_recv()
        la_o[...] = S.la[...]

    def low_5():
        st.low_g[0].wait_recv()
        rows = []
        for b in range(8):
            v = jnp.concatenate([S.low_p[0, b], S.low_p[1, b]], axis=0).astype(F32)
            rows.append(unpack(v))
        total = None
        for i in range(BATCHES):
            low = jnp.concatenate([v[i * BLK : (i + 1) * BLK] for v in rows], axis=0)
            v = dot((0.5 * low).T.astype(BF16), whole(S.cot, i))
            total = v if total is None else total + v
        lb_o[...] = total

    a1(0)
    a1(1)
    a2(0)
    a1(2)
    a2(1)
    a3(0)
    a1(3)
    a2(2)
    a3(1)
    a4(0)
    back_send()
    a2(3)
    a3(2)
    a4(1)
    b2(0)
    a3(3)
    a4(2)
    b2(1)
    b3(0)
    a4(3)
    b2(2)
    b3(1)
    b4(0)
    b2(3)
    b3(2)
    low_1()
    b4(1)
    c2(0)
    b3(3)
    b4(2)
    low_2()
    c2(1)
    b4(3)
    c2(2)
    la_2()
    c3(0)
    low_3()
    c2(3)
    c3(1)
    la_3()
    low_4()
    c4(0)
    c3(2)
    c4(1)
    low_5()
    c3(3)
    c4(2)
    c4(3)
    for cp, cond in sent:
        if cond is None:
            cp.wait_send()
        else:
            pl.when(cond)(cp.wait_send)


def hand_over(*refs):
    for src, dst in zip(refs[:3], refs[3:]):
        dst[...] = src[...]


def shards(tok, cot, gate_w, up_w, down_w, down_a, down_b):
    any_ = pl.BlockSpec(memory_space=pl.ANY)
    vmem = pl.BlockSpec(memory_space=pltpu.VMEM)
    grad_in, grad_a, grad_b = pl.pallas_call(
        kernel,
        out_shape=(
            jax.ShapeDtypeStruct((16, FEAT), BF16),
            jax.ShapeDtypeStruct((RANK, HID), F32),
            jax.ShapeDtypeStruct((RANK, FEAT), F32),
        ),
        in_specs=[any_] * 7,
        out_specs=(vmem, vmem, vmem),
        scratch_shapes=scratch_spec()[0]
        + [
            pltpu.SemaphoreType.DMA((N_COPIES,)),
            pltpu.SemaphoreType.DMA((N_COPIES,)),
            pltpu.SemaphoreType.DMA((N_LOADS,)),
        ],
        compiler_params=pltpu.CompilerParams(
            collective_id=0, has_side_effects=True, vmem_limit_bytes=60 * 2**20
        ),
    )(tok.reshape(8, 4, BLK, FEAT), cot.reshape(8, 4, BLK, FEAT), gate_w, up_w, down_w, down_a.T, down_b)
    grad_in, grad_a, grad_b = pl.pallas_call(
        hand_over,
        out_shape=(
            jax.ShapeDtypeStruct((16, FEAT), BF16),
            jax.ShapeDtypeStruct((RANK, HID), F32),
            jax.ShapeDtypeStruct((RANK, FEAT), F32),
        ),
        in_specs=[vmem] * 3,
        out_specs=(vmem, vmem, vmem),
    )(grad_in, grad_a, grad_b)
    return grad_in, grad_a.T, grad_b


def solution(mesh):
    return jax.shard_map(
        shards,
        mesh=mesh,
        in_specs=(
            P(None, "pipe"),
            P(None, "pipe"),
            P("pipe", "fsdp"),
            P("pipe", "fsdp"),
            P("fsdp", "pipe"),
            P("fsdp", None),
            P(None, "pipe"),
        ),
        out_specs=(P("fsdp", "pipe"), P("fsdp", None), P(None, "pipe")),
        check_vma=False,
    )
```

```python
import jax
import jax.numpy as jnp
from jax import lax
from jax.experimental import pallas as pl
from jax.experimental.pallas import tpu as pltpu
from jax.sharding import PartitionSpec as P

F32 = jnp.float32
BF16 = jnp.bfloat16
MESH = pl.DeviceIdType.MESH

TOK = 512
FEAT = 1536
HID = 896
RANK = 64
BATCHES = 4
ROWS = 128
BLK = 16
XW = 512
YW = 384
SPLIT = (0, 640, 1152)
N_COPIES = 240
N_LOADS = 20


def dot(a, b):
    return jnp.dot(a, b, preferred_element_type=F32)


def dot_t(a, b):
    return lax.dot_general(a, b, (((1,), (1,)), ((), ())), preferred_element_type=F32)


def dot_lead(a, b):
    return lax.dot_general(a, b, (((0,), (0,)), ((), ())), preferred_element_type=F32)


def pack(v):
    return jnp.concatenate([v[:32], v[32:]], axis=1)


def unpack(v):
    return jnp.concatenate([v[:, :64], v[:, 64:]], axis=0)


class Bag:
    pass


class Copies:
    def __getattr__(self, name):
        made = {}
        setattr(self, name, made)
        return made


def n_parts(i):
    return 2 if i == BATCHES - 1 else 1


def scratch_spec():
    specs = []
    v = Bag()

    def new(shape, dtype):
        specs.append(pltpu.VMEM(shape, dtype))
        return len(specs) - 1

    n = BATCHES
    v.tok = new((n, 8, BLK, FEAT), BF16)
    v.cot = new((n, 8, BLK, FEAT), BF16)
    v.gw = new((FEAT, HID), BF16)
    v.uw = new((FEAT, HID), BF16)
    v.dw = new((HID, FEAT), BF16)
    v.down_a = new((RANK, HID), BF16)
    v.down_b = new((RANK, FEAT), BF16)
    wide = 3 * XW
    v.xpart = new((n, ROWS, wide), F32)
    v.xfd_s = new((n, 4, BLK, wide), BF16)
    v.xfd_r = new((n, 4, BLK, wide), BF16)
    v.xc_s = new((n, 2, BLK, wide), BF16)
    v.xc_r = new((n, 2, BLK, wide), BF16)
    v.xsum = new((n, 2, BLK, wide), F32)
    v.xy_s = new((n, BLK, wide), BF16)
    v.xy_r = new((n, BLK, wide), BF16)
    v.xgrad = new((n, ROWS, 2 * XW), BF16)
    wide = 3 * YW
    v.ypart = new((n, ROWS, wide), F32)
    v.yy_s = new((n, 64, wide), BF16)
    v.yy_r = new((n, 64, wide), BF16)
    v.ysum = new((n, 64, wide), F32)
    v.yfd_s = new((n, 2, BLK, wide), BF16)
    v.yfd_r = new((n, 2, BLK, wide), BF16)
    v.yc_s = new((n, BLK, wide), BF16)
    v.yc_r = new((n, BLK, wide), BF16)
    v.ygrad = new((n, ROWS, 2 * YW), BF16)
    v.hidden = new((TOK // 8, HID), BF16)
    v.acc = new((n, ROWS, FEAT), F32)
    v.back = new((n, 8, BLK, RANK), F32)
    v.back_s = new((8, 32, 128), BF16)
    v.back_r = new((8, 32, 128), BF16)
    v.la_s = new((RANK, HID), F32)
    v.la_r = new((8, 8, HID), F32)
    v.la = new((RANK, HID), F32)
    v.low_s = new((32, 128), F32)
    v.low_cr = new((32, 128), F32)
    v.low_h = new((16, 128), F32)
    v.low_zr = new((16, 16, 128), F32)
    v.low_p = new((2, 8, 16, 128), BF16)
    v.core_r = new((n, ROWS, FEAT), F32)
    v.z_s = new((n, 8, BLK, FEAT), BF16)
    v.z_r = new((n, 8, BLK, FEAT), BF16)
    v.yh_s = new((n, BLK, FEAT), F32)
    v.yh_r = new((n, BLK, FEAT), F32)
    return specs, v


def kernel(*refs):
    specs, places = scratch_spec()
    tok_h, cot_h, gw_h, uw_h, dw_h, a_h, b_h, gi_o, la_o, lb_o = refs[:10]
    held = refs[10 : 10 + len(specs)]
    send_sems, recv_sems, load_sems = refs[10 + len(specs) :]
    S = Bag()
    for name, place in vars(places).items():
        setattr(S, name, held[place])

    p = lax.axis_index("pipe")
    f = lax.axis_index("fsdp")
    x = lax.rem(p, 4)
    y = lax.div(p, 4)
    z = lax.div(f, 4)
    yh = lax.rem(lax.div(f, 2), 2)
    core = lax.rem(f, 2)
    chip = lax.div(f, 2)
    x_p, x_m, x_f = lax.rem(x + 1, 4), lax.rem(x + 3, 4), lax.rem(x + 2, 4)

    def pipe(i):
        return {"pipe": i}

    def fsdp(i):
        return {"fsdp": i}

    to_xp = pipe(y * 4 + x_p)
    to_xm = pipe(y * 4 + x_m)
    to_y = pipe((1 - y) * 4 + x)
    to_core = fsdp(f + 1 - 2 * core)
    to_yh = fsdp(f + 2 - 4 * yh)

    count = [0]
    sent = []

    def remote(src, dst, dev):
        i = count[0]
        count[0] += 1
        return pltpu.make_async_remote_copy(
            src_ref=src,
            dst_ref=dst,
            send_sem=send_sems.at[i],
            recv_sem=recv_sems.at[i],
            device_id=dev,
            device_id_type=MESH,
        )

    entered = []

    def go(cp, cond=None):
        if not entered:
            pl.semaphore_wait(barrier, len(peers))
            entered.append(True)
        cp.start()
        sent.append((cp, cond))
        return cp

    loads = {}

    def load(key, dst, src):
        cp = pltpu.make_async_copy(src, dst, load_sems.at[len(loads)])
        cp.start()
        loads[key] = cp

    XC, YC = slice(0, XW), slice(XW, HID)
    xcols, ycols = pl.ds(0, XW), pl.ds(XW, YW)
    TOKENS, COT, GATE_W, UP_W, DOWN_W, DOWN_A, DOWN_B = range(7)
    load((TOKENS, 0), S.tok.at[0], tok_h.at[:, 0])
    load((GATE_W, 0), S.gw.at[:, xcols], gw_h.at[:, xcols])
    load((UP_W, 0), S.uw.at[:, xcols], uw_h.at[:, xcols])
    load((COT, 0), S.cot.at[0], cot_h.at[:, 0])
    load(DOWN_B, S.down_b, b_h)
    load(DOWN_A, S.down_a, a_h)
    load((DOWN_W, 0), S.dw.at[xcols], dw_h.at[xcols])
    load((GATE_W, 1), S.gw.at[:, ycols], gw_h.at[:, ycols])
    load((UP_W, 1), S.uw.at[:, ycols], uw_h.at[:, ycols])
    load((DOWN_W, 1), S.dw.at[ycols], dw_h.at[ycols])
    for i in range(1, BATCHES):
        load((TOKENS, i), S.tok.at[i], tok_h.at[:, i])
        load((COT, i), S.cot.at[i], cot_h.at[:, i])

    barrier = pltpu.get_barrier_semaphore()
    peers = [pipe(lax.rem(p + j, 8)) for j in range(1, 8)]
    peers += [to_core]
    peers += [fsdp(lax.rem(chip + j, 16) * 2 + core) for j in range(1, 16)]
    for dev in peers:
        pl.semaphore_signal(barrier, inc=1, device_id=dev, device_id_type=MESH)

    def block(x_, y_):
        return pl.ds(pl.multiple_of((y_ * 4 + x_) * BLK, BLK), BLK)

    def quarter(x_):
        return pl.ds(pl.multiple_of(x_ * BLK, BLK), BLK)

    def half(y_):
        return pl.ds(pl.multiple_of(y_ * 64, 64), 64)

    def side(k):
        return slice(SPLIT[k], SPLIT[k + 1])

    def side_d(k):
        return pl.ds(SPLIT[k], SPLIT[k + 1] - SPLIT[k])

    st = Copies()

    def whole(ref, i):
        return ref[i].reshape(ROWS, FEAT)

    def products(i, part, cols, w):
        tok, cot = whole(S.tok, i), whole(S.cot, i)
        part[i, :, 0:w] = dot(tok, S.gw[:, cols])
        part[i, :, w : 2 * w] = dot(tok, S.uw[:, cols])
        back = (0.5 * S.back[i].reshape(ROWS, RANK)).astype(BF16)
        part[i, :, 2 * w :] = dot_t(cot, S.dw[cols, :]) + dot(back, S.down_a[:, cols])

    waited = set()

    def need(*keys):
        for key in keys:
            if key not in waited:
                waited.add(key)
                loads[key].wait()

    def back_of(i):
        need((COT, i), DOWN_B)
        if (RANK, i) not in waited:
            waited.add((RANK, i))
            S.back[i] = dot_t(whole(S.cot, i), S.down_b[...]).reshape(8, BLK, RANK)

    def a1x(i):
        need((TOKENS, i), (GATE_W, 0), (UP_W, 0), (DOWN_W, 0), DOWN_A)
        back_of(i)
        products(i, S.xpart, XC, XW)
        plan = ((x_f, 0, to_xp), (x_f, 1, to_xm), (x_p, 1, to_xp), (x_m, 0, to_xm))
        for k, (bx, by, dev) in enumerate(plan):
            S.xfd_s[i, k] = S.xpart[i, block(bx, by), :].astype(BF16)
            st.xfd[i, k] = go(remote(S.xfd_s.at[i, k], S.xfd_r.at[i, k], dev))

    def a1y(i):
        need((TOKENS, i), (GATE_W, 1), (UP_W, 1), (DOWN_W, 1), DOWN_A)
        back_of(i)
        products(i, S.ypart, YC, YW)
        S.yy_s[i] = S.ypart[i, half(1 - y), :].astype(BF16)
        st.yy[i] = go(remote(S.yy_s.at[i], S.yy_r.at[i], to_y))

    def a2x(i):
        for k, rows, dev in ((0, block(x_p, 0), to_xp), (1, block(x_m, 1), to_xm)):
            st.xfd[i, k].wait_recv()
            S.xc_s[i, k] = (S.xpart[i, rows, :] + S.xfd_r[i, k].astype(F32)).astype(BF16)
            st.xc[i, k] = go(remote(S.xc_s.at[i, k], S.xc_r.at[i, k], dev))

    def a2y(i):
        st.yy[i].wait_recv()
        S.ysum[i] = S.ypart[i, half(y), :] + S.yy_r[i].astype(F32)
        plan = ((0, 0, x_f, to_xp), (0, 1, x_f, to_xm), (1, 1, x_p, to_xp), (1, 0, x_m, to_xm))
        for k, s, bx, dev in plan:
            S.yfd_s[i, k, :, side(s)] = S.ysum[i, quarter(bx), side(s)].astype(BF16)
            st.yfd[i, k, s] = go(
                remote(
                    S.yfd_s.at[i, k, :, side_d(s)], S.yfd_r.at[i, k, :, side_d(s)], dev
                )
            )

    def a3x(i):
        for k in (2, 3):
            st.xfd[i, k].wait_recv()
        for k in (0, 1):
            st.xc[i, k].wait_recv()
        for k in (0, 1):
            S.xsum[i, k] = (
                S.xpart[i, block(x, k), :]
                + S.xfd_r[i, 3 - k].astype(F32)
                + S.xc_r[i, k].astype(F32)
            )
        S.xy_s[i] = S.xsum[i, 1 - y].astype(BF16)
        st.xy[i] = go(remote(S.xy_s.at[i], S.xy_r.at[i], to_y))

    def a3y(i):
        for s, bx, dev in ((0, x_p, to_xp), (1, x_m, to_xm)):
            st.yfd[i, 0, s].wait_recv()
            S.yc_s[i, :, side(s)] = (
                S.ysum[i, quarter(bx), side(s)] + S.yfd_r[i, 0, :, side(s)].astype(F32)
            ).astype(BF16)
            st.yc[i, s] = go(
                remote(S.yc_s.at[i, :, side_d(s)], S.yc_r.at[i, :, side_d(s)], dev)
            )

    def activate(i, total, w, grad, cols):
        gate, up, hg = total[:, :w], total[:, w : 2 * w], total[:, 2 * w :]
        sig = jax.nn.sigmoid(gate)
        silu = gate * sig
        mine = block(x, y)
        grad[i, mine, 0:w] = (hg * up * sig * (1.0 + gate * (1.0 - sig))).astype(BF16)
        grad[i, mine, w : 2 * w] = (hg * silu).astype(BF16)
        S.hidden[i * BLK : (i + 1) * BLK, cols] = (silu * up).astype(BF16)

    def a4x(i):
        st.xy[i].wait_recv()
        activate(i, S.xsum[i, y] + S.xy_r[i].astype(F32), XW, S.xgrad, XC)
        slot = S.xgrad.at[i, block(x, y)]
        st.xown_y[i] = go(remote(slot, slot, to_y))
        st.xown_p[i] = go(remote(slot, slot, to_xp))
        st.xown_m[i] = go(remote(slot, slot, to_xm))

    def a4y(i):
        for s in (0, 1):
            st.yfd[i, 1, s].wait_recv()
            st.yc[i, s].wait_recv()
        total = (
            S.ysum[i, quarter(x), :] + S.yfd_r[i, 1].astype(F32) + S.yc_r[i].astype(F32)
        )
        activate(i, total, YW, S.ygrad, YC)
        slot = S.ygrad.at[i, block(x, y)]
        st.yown_p[i] = go(remote(slot, slot, to_xp))
        st.yown_m[i] = go(remote(slot, slot, to_xm))
        st.yown_y[i] = go(remote(slot, slot, to_y))

    def b2x(i):
        st.xown_y[i].wait_recv()
        slot = S.xgrad.at[i, block(x, 1 - y)]
        st.xoth_p[i] = go(remote(slot, slot, to_xp))
        st.xoth_m[i] = go(remote(slot, slot, to_xm))

    def b2y(i):
        left, right = pl.ds(0, YW), pl.ds(YW, YW)
        st.yown_p[i].wait_recv()
        part = S.ygrad.at[i, block(x_m, y), left]
        st.yfar_p[i] = go(remote(part, part, to_xp))
        slot = S.ygrad.at[i, block(x_m, y)]
        st.yy_m[i] = go(remote(slot, slot, to_y))
        st.yown_m[i].wait_recv()
        part = S.ygrad.at[i, block(x_p, y), right]
        st.yfar_m[i] = go(remote(part, part, to_xm))
        slot = S.ygrad.at[i, block(x_p, y)]
        st.yy_p[i] = go(remote(slot, slot, to_y))

    def b3x(i):
        st.xown_p[i].wait_recv()
        slot = S.xgrad.at[i, block(x_m, y)]
        st.xfar_p[i] = go(remote(slot, slot, to_xp))
        st.xoth_m[i].wait_recv()
        slot = S.xgrad.at[i, block(x_p, 1 - y)]
        st.xfar_m[i] = go(remote(slot, slot, to_xm))

    def b3y(i):
        st.yfar_p[i].wait_recv()
        st.yfar_m[i].wait_recv()
        slot = S.ygrad.at[i, block(x_f, y)]
        st.yy_f[i] = go(remote(slot, slot, to_y))

    def owner_core(i):
        return i % 2

    def owner_yh(i):
        return i // 2

    def part_cols(i, q):
        w = FEAT // n_parts(i)
        return slice(q * w, (q + 1) * w), pl.ds(q * w, w)

    def b4x(i):
        for copies in (st.xown_m, st.xoth_p, st.xfar_p, st.xfar_m):
            copies[i].wait_recv()
        v = dot_t(S.xgrad[i, :, 0:XW], S.gw[:, XC]) + dot_t(S.xgrad[i, :, XW:], S.uw[:, XC])
        S.acc[i] = v

    def b4y(i):
        for copies in (st.yown_y, st.yy_m, st.yy_p, st.yy_f):
            copies[i].wait_recv()
        away = core != owner_core(i)
        for q in range(n_parts(i)):
            cols, cols_d = part_cols(i, q)
            S.acc[i, :, cols] += dot_t(S.ygrad[i, :, 0:YW], S.gw[cols, YC]) + dot_t(
                S.ygrad[i, :, YW:], S.uw[cols, YC]
            )
            st.core[i, q] = remote(S.acc.at[i, :, cols_d], S.core_r.at[i, :, cols_d], to_core)
            pl.when(away)(lambda q=q: go(st.core[i, q], away) and None)

    def z_rows(j):
        return pl.ds(pl.multiple_of(lax.rem(z + j, 8) * BLK, BLK), BLK)

    def c2(i, q=0):
        here = core == owner_core(i)
        cols, cols_d = part_cols(i, q)
        for j in range(1, 8):
            dev = fsdp(lax.rem(f + 4 * j, 32))
            st.z[i, q, j] = remote(S.z_s.at[i, j, :, cols_d], S.z_r.at[i, j, :, cols_d], dev)

        @pl.when(here)
        def _():
            st.core[i, q].wait_recv()
            for j in (4, 3, 5, 2, 6, 1, 7):
                rows = z_rows(j)
                S.z_s[i, j, :, cols] = (
                    S.acc[i, rows, cols] + S.core_r[i, rows, cols]
                ).astype(BF16)
                go(st.z[i, q, j], here)

    def c3(i, q=0):
        here = core == owner_core(i)
        away = jnp.logical_and(here, yh != owner_yh(i))
        cols, cols_d = part_cols(i, q)
        st.yh[i, q] = remote(S.yh_s.at[i, :, cols_d], S.yh_r.at[i, :, cols_d], to_yh)

        @pl.when(here)
        def _():
            rows = z_rows(0)
            total = S.acc[i, rows, cols] + S.core_r[i, rows, cols]
            for j in (1, 7, 2, 6, 3, 5, 4):
                st.z[i, q, j].wait_recv()
                total = total + S.z_r[i, j, :, cols].astype(F32)
            S.yh_s[i, :, cols] = total

        @pl.when(away)
        def _():
            go(st.yh[i, q], away)

    def c4(i, q=0):
        cols, _ = part_cols(i, q)

        @pl.when(jnp.logical_and(core == owner_core(i), yh == owner_yh(i)))
        def _():
            st.yh[i, q].wait_recv()
            gi_o[:, cols] = (S.yh_s[i, :, cols] + S.yh_r[i, :, cols]).astype(BF16)

    def back_send():
        for b in range(8):
            rows = jnp.concatenate([S.back[i, b] for i in range(BATCHES)], axis=0)
            S.back_s[b] = pack(rows).astype(BF16)
        for j in range(1, 8):
            dst = lax.rem(p + j, 8)
            st.back[j] = go(remote(S.back_s.at[dst], S.back_r.at[j], pipe(dst)))

    def low_1():
        S.low_s[...] = pack(dot_t(S.down_a[...], S.hidden[...]))
        st.low_c[0] = go(remote(S.low_s, S.low_cr, to_core))

    def la_1():
        total = S.back_s[p].astype(F32)
        for j in range(1, 8):
            st.back[j].wait_recv()
            total = total + S.back_r[j].astype(F32)
        back = (0.5 * unpack(total)).astype(BF16)
        S.la_s[...] = dot_lead(back, S.hidden[...])
        for j in range(1, 8):
            dst = lax.rem(p + j, 8)
            rows = S.la_s.at[pl.ds(pl.multiple_of(dst * 8, 8), 8)]
            st.la[j] = go(remote(rows, S.la_r.at[j], pipe(dst)))

    def low_2():
        st.low_c[0].wait_recv()
        rows = pl.ds(pl.multiple_of(core * 16, 16), 16)
        S.low_h[...] = S.low_s[rows, :] + S.low_cr[rows, :]
        for j in range(1, 16):
            dev = fsdp(lax.rem(chip + j, 16) * 2 + core)
            st.low_z[j] = go(remote(S.low_h, S.low_zr.at[j], dev))

    def la_2():
        mine = pl.ds(pl.multiple_of(p * 8, 8), 8)
        total = S.la_s[mine, :]
        for j in range(1, 8):
            st.la[j].wait_recv()
            total = total + S.la_r[j]
        S.la[mine, :] = total
        slot = S.la.at[mine]
        for j in range(1, 8):
            st.la_g[j] = go(remote(slot, slot, pipe(lax.rem(p + j, 8))))

    def low_3():
        total = S.low_h[...]
        for j in range(1, 16):
            st.low_z[j].wait_recv()
            total = total + S.low_zr[j]
        S.low_p[core, p] = total.astype(BF16)
        slot = S.low_p.at[core, p]
        for j in range(1, 8):
            st.low_p[j] = go(remote(slot, slot, pipe(lax.rem(p + j, 8))))

    def low_4():
        for j in range(1, 8):
            st.low_p[j].wait_recv()
        slot = S.low_p.at[core]
        st.low_g[0] = go(remote(slot, slot, to_core))

    def la_3():
        for j in range(1, 8):
            st.la_g[j].wait_recv()
        la_o[...] = S.la[...]

    def low_5():
        st.low_g[0].wait_recv()
        total = None
        for b in range(8):
            v = jnp.concatenate([S.low_p[0, b], S.low_p[1, b]], axis=0).astype(F32)
            low = (0.5 * unpack(v)).astype(BF16)
            v = dot(low, S.cot[:, b].reshape(64, FEAT))
            total = v if total is None else total + v
        lb_o[...] = total

    a1x(0)
    a1y(1)
    a1x(2)
    a1y(0)
    a2x(0)
    a1x(1)
    a1y(2)
    a2x(2)
    a1x(3)
    a2y(0)
    a3x(0)
    a1y(3)
    a2x(1)
    a2y(1)
    a3y(0)
    a2x(3)
    a4x(0)
    a2y(2)
    a3x(1)
    a4y(0)
    a3x(2)
    a2y(3)
    a3y(1)
    b2x(0)
    a3x(3)
    a4x(1)
    b2y(0)
    a3y(3)
    a3y(2)
    a4y(1)
    b3x(0)
    a4x(2)
    b2x(1)
    b3y(0)
    a4x(3)
    a4y(3)
    a4y(2)
    low_1()
    b2y(1)
    b4x(0)
    b2x(2)
    b4y(0)
    b3x(1)
    low_2()
    b2x(3)
    b3y(1)
    b2y(2)
    b2y(3)
    c2(0)
    b3x(2)
    b4x(1)
    b4y(1)
    b3x(3)
    b3y(2)
    back_send()
    b3y(3)
    b4x(2)
    c2(1)
    b4y(2)
    b4x(3)
    low_3()
    c2(2)
    c3(0)
    la_1()
    b4y(3)
    c2(3, 0)
    c4(0)
    c3(1)
    la_2()
    c2(3, 1)
    low_4()
    c4(1)
    c3(2)
    c3(3, 0)
    c3(3, 1)
    c4(2)
    la_3()
    low_5()
    c4(3, 0)
    c4(3, 1)
    for cp, cond in sent:
        if cond is None:
            cp.wait_send()
        else:
            pl.when(cond)(cp.wait_send)


def hand_over(*refs):
    for src, dst in zip(refs[:3], refs[3:]):
        dst[...] = src[...]


def shards(tok, cot, gate_w, up_w, down_w, down_a, down_b):
    any_ = pl.BlockSpec(memory_space=pl.ANY)
    vmem = pl.BlockSpec(memory_space=pltpu.VMEM)
    grad_in, grad_a, grad_b = pl.pallas_call(
        kernel,
        out_shape=(
            jax.ShapeDtypeStruct((16, FEAT), BF16),
            jax.ShapeDtypeStruct((RANK, HID), F32),
            jax.ShapeDtypeStruct((RANK, FEAT), F32),
        ),
        in_specs=[any_] * 7,
        out_specs=(vmem, vmem, vmem),
        scratch_shapes=scratch_spec()[0]
        + [
            pltpu.SemaphoreType.DMA((N_COPIES,)),
            pltpu.SemaphoreType.DMA((N_COPIES,)),
            pltpu.SemaphoreType.DMA((N_LOADS,)),
        ],
        compiler_params=pltpu.CompilerParams(
            collective_id=0, has_side_effects=True, vmem_limit_bytes=60 * 2**20
        ),
    )(tok.reshape(8, 4, BLK, FEAT), cot.reshape(8, 4, BLK, FEAT), gate_w, up_w, down_w, down_a.T, down_b)
    grad_in, grad_a, grad_b = pl.pallas_call(
        hand_over,
        out_shape=(
            jax.ShapeDtypeStruct((16, FEAT), BF16),
            jax.ShapeDtypeStruct((RANK, HID), F32),
            jax.ShapeDtypeStruct((RANK, FEAT), F32),
        ),
        in_specs=[vmem] * 3,
        out_specs=(vmem, vmem, vmem),
    )(grad_in, grad_a, grad_b)
    return grad_in, grad_a.T, grad_b


def solution(mesh):
    return jax.shard_map(
        shards,
        mesh=mesh,
        in_specs=(
            P(None, "pipe"),
            P(None, "pipe"),
            P("pipe", "fsdp"),
            P("pipe", "fsdp"),
            P("fsdp", "pipe"),
            P("fsdp", None),
            P(None, "pipe"),
        ),
        out_specs=(P("fsdp", "pipe"), P("fsdp", None), P(None, "pipe")),
        check_vma=False,
    )
```

```python
import jax
import jax.numpy as jnp
from jax import lax
from jax.experimental import pallas as pl
from jax.experimental.pallas import tpu as pltpu
from jax.sharding import PartitionSpec as P

F32 = jnp.float32
BF16 = jnp.bfloat16
MESH = pl.DeviceIdType.MESH

TOK = 512
FEAT = 1536
HID = 896
RANK = 64
BATCHES = 4
ROWS = 128
BLK = 16
XW = 512
YW = 384
SPLIT = (0, 640, 1152)
N_COPIES = 260
N_LOADS = 20


def dot(a, b):
    return jnp.dot(a, b, preferred_element_type=F32)


def dot_t(a, b):
    return lax.dot_general(a, b, (((1,), (1,)), ((), ())), preferred_element_type=F32)


def dot_lead(a, b):
    return lax.dot_general(a, b, (((0,), (0,)), ((), ())), preferred_element_type=F32)


def pack(v):
    return jnp.concatenate([v[:32], v[32:]], axis=1)


def unpack(v):
    return jnp.concatenate([v[:, :64], v[:, 64:]], axis=0)


class Bag:
    pass


class Copies:
    def __getattr__(self, name):
        made = {}
        setattr(self, name, made)
        return made


def n_parts(i):
    return 2 if i == BATCHES - 1 else 1


def scratch_spec():
    specs = []
    v = Bag()

    def new(shape, dtype):
        specs.append(pltpu.VMEM(shape, dtype))
        return len(specs) - 1

    n = BATCHES
    v.tok = new((n, 8, BLK, FEAT), BF16)
    v.cot = new((n, 8, BLK, FEAT), BF16)
    v.wx = new((FEAT, 2 * XW), BF16)
    v.wy = new((FEAT, 2 * YW), BF16)
    v.dw = new((HID, FEAT), BF16)
    v.down_a = new((RANK, HID), BF16)
    v.down_b = new((RANK, FEAT), BF16)
    wide = 3 * XW
    v.xpart = new((n, ROWS, wide), F32)
    v.xfd_s = new((n, 4, BLK, wide), BF16)
    v.xfd_r = new((n, 4, BLK, wide), BF16)
    v.xc_s = new((n, 2, BLK, wide), BF16)
    v.xc_r = new((n, 2, BLK, wide), BF16)
    v.xsum = new((n, 2, BLK, wide), F32)
    v.xy_s = new((n, BLK, wide), BF16)
    v.xy_r = new((n, BLK, wide), BF16)
    v.xgrad = new((n, ROWS, 2 * XW), BF16)
    wide = 3 * YW
    v.ypart = new((n, ROWS, wide), F32)
    v.yy_s = new((n, 64, wide), BF16)
    v.yy_r = new((n, 64, wide), BF16)
    v.ysum = new((n, 64, wide), F32)
    v.yfd_s = new((n, 2, BLK, wide), BF16)
    v.yfd_r = new((n, 2, BLK, wide), BF16)
    v.yc_s = new((n, BLK, wide), BF16)
    v.yc_r = new((n, BLK, wide), BF16)
    v.ygrad = new((n, ROWS, 2 * YW), BF16)
    v.hidden = new((TOK // 8, HID), BF16)
    v.acc = new((n, ROWS, FEAT), F32)
    v.back = new((n, 8, BLK, RANK), F32)
    v.back_s = new((8, 32, 128), BF16)
    v.back_r = new((8, 32, 128), BF16)
    v.la_s = new((RANK, HID), F32)
    v.la_r = new((8, 8, HID), F32)
    v.la = new((RANK, HID), F32)
    v.low_s = new((32, 128), F32)
    v.low_cr = new((32, 128), F32)
    v.low_h = new((16, 128), F32)
    v.low_zr = new((16, 16, 128), F32)
    v.low_p = new((2, 8, 16, 128), BF16)
    v.core_r = new((n, ROWS, FEAT), F32)
    v.z_s = new((n, 8, BLK, FEAT), BF16)
    v.z_r = new((n, 8, BLK, FEAT), BF16)
    v.other_r = new((n, 8, BLK, FEAT), BF16)
    v.yh_s = new((n, BLK, FEAT), F32)
    v.yh_r = new((n, BLK, FEAT), F32)
    return specs, v


def kernel(*refs):
    specs, places = scratch_spec()
    tok_h, cot_h, gw_h, uw_h, dw_h, a_h, b_h, gi_o, la_o, lb_o = refs[:10]
    held = refs[10 : 10 + len(specs)]
    send_sems, recv_sems, load_sems = refs[10 + len(specs) :]
    S = Bag()
    for name, place in vars(places).items():
        setattr(S, name, held[place])

    p = lax.axis_index("pipe")
    f = lax.axis_index("fsdp")
    x = lax.rem(p, 4)
    y = lax.div(p, 4)
    z = lax.div(f, 4)
    yh = lax.rem(lax.div(f, 2), 2)
    core = lax.rem(f, 2)
    chip = lax.div(f, 2)
    x_p, x_m, x_f = lax.rem(x + 1, 4), lax.rem(x + 3, 4), lax.rem(x + 2, 4)

    def pipe(i):
        return {"pipe": i}

    def fsdp(i):
        return {"fsdp": i}

    to_xp = pipe(y * 4 + x_p)
    to_xm = pipe(y * 4 + x_m)
    to_y = pipe((1 - y) * 4 + x)
    to_core = fsdp(f + 1 - 2 * core)
    to_yh = fsdp(f + 2 - 4 * yh)

    count = [0]
    sent = []

    def remote(src, dst, dev):
        i = count[0]
        count[0] += 1
        return pltpu.make_async_remote_copy(
            src_ref=src,
            dst_ref=dst,
            send_sem=send_sems.at[i],
            recv_sem=recv_sems.at[i],
            device_id=dev,
            device_id_type=MESH,
        )

    entered = []

    def go(cp, cond=None):
        if not entered:
            pl.semaphore_wait(barrier, len(peers))
            entered.append(True)
        cp.start()
        sent.append((cp, cond))
        return cp

    loads = {}

    def load(key, dst, src):
        cp = pltpu.make_async_copy(src, dst, load_sems.at[len(loads)])
        cp.start()
        loads[key] = cp

    XC, YC = slice(0, XW), slice(XW, HID)
    xcols, ycols = pl.ds(0, XW), pl.ds(XW, YW)
    TOKENS, COT, GATE_W, UP_W, DOWN_W, DOWN_A, DOWN_B = range(7)
    load((TOKENS, 0), S.tok.at[0], tok_h.at[:, 0])
    load((GATE_W, 0), S.wx.at[:, pl.ds(0, XW)], gw_h.at[:, xcols])
    load((UP_W, 0), S.wx.at[:, pl.ds(XW, XW)], uw_h.at[:, xcols])
    load((COT, 0), S.cot.at[0], cot_h.at[:, 0])
    load(DOWN_B, S.down_b, b_h)
    load(DOWN_A, S.down_a, a_h)
    load((DOWN_W, 0), S.dw.at[xcols], dw_h.at[xcols])
    load((GATE_W, 1), S.wy.at[:, pl.ds(0, YW)], gw_h.at[:, ycols])
    load((UP_W, 1), S.wy.at[:, pl.ds(YW, YW)], uw_h.at[:, ycols])
    load((DOWN_W, 1), S.dw.at[ycols], dw_h.at[ycols])
    for i in range(1, BATCHES):
        load((TOKENS, i), S.tok.at[i], tok_h.at[:, i])
        load((COT, i), S.cot.at[i], cot_h.at[:, i])

    barrier = pltpu.get_barrier_semaphore()
    peers = [pipe(lax.rem(p + j, 8)) for j in range(1, 8)]
    peers += [to_core]
    peers += [fsdp(lax.rem(chip + j, 16) * 2 + core) for j in range(1, 16)]
    for dev in peers:
        pl.semaphore_signal(barrier, inc=1, device_id=dev, device_id_type=MESH)

    def block(x_, y_):
        return pl.ds(pl.multiple_of((y_ * 4 + x_) * BLK, BLK), BLK)

    def quarter(x_):
        return pl.ds(pl.multiple_of(x_ * BLK, BLK), BLK)

    def half(y_):
        return pl.ds(pl.multiple_of(y_ * 64, 64), 64)

    def side(k):
        return slice(SPLIT[k], SPLIT[k + 1])

    def side_d(k):
        return pl.ds(SPLIT[k], SPLIT[k + 1] - SPLIT[k])

    st = Copies()

    def whole(ref, i):
        return ref[i].reshape(ROWS, FEAT)

    def products(i, part, weights, cols, w):
        tok, cot = whole(S.tok, i), whole(S.cot, i)
        part[i, :, 0 : 2 * w] = dot(tok, weights[...])
        back = (0.5 * S.back[i].reshape(ROWS, RANK)).astype(BF16)
        part[i, :, 2 * w :] = dot_t(cot, S.dw[cols, :]) + dot(back, S.down_a[:, cols])

    waited = set()

    def need(*keys):
        for key in keys:
            if key not in waited:
                waited.add(key)
                loads[key].wait()

    def back_of(i):
        need((COT, i), DOWN_B)
        if (RANK, i) not in waited:
            waited.add((RANK, i))
            S.back[i] = dot_t(whole(S.cot, i), S.down_b[...]).reshape(8, BLK, RANK)

    def a1x(i):
        need((TOKENS, i), (GATE_W, 0), (UP_W, 0), (DOWN_W, 0), DOWN_A)
        back_of(i)
        products(i, S.xpart, S.wx, XC, XW)
        plan = ((x_f, 0, to_xp), (x_f, 1, to_xm), (x_p, 1, to_xp), (x_m, 0, to_xm))
        for k, (bx, by, dev) in enumerate(plan):
            S.xfd_s[i, k] = S.xpart[i, block(bx, by), :].astype(BF16)
            st.xfd[i, k] = go(remote(S.xfd_s.at[i, k], S.xfd_r.at[i, k], dev))

    def a1y(i):
        need((TOKENS, i), (GATE_W, 1), (UP_W, 1), (DOWN_W, 1), DOWN_A)
        back_of(i)
        products(i, S.ypart, S.wy, YC, YW)
        S.yy_s[i] = S.ypart[i, half(1 - y), :].astype(BF16)
        st.yy[i] = go(remote(S.yy_s.at[i], S.yy_r.at[i], to_y))

    def a2x(i):
        for k, rows, dev in ((0, block(x_p, 0), to_xp), (1, block(x_m, 1), to_xm)):
            st.xfd[i, k].wait_recv()
            S.xc_s[i, k] = (S.xpart[i, rows, :] + S.xfd_r[i, k].astype(F32)).astype(BF16)
            st.xc[i, k] = go(remote(S.xc_s.at[i, k], S.xc_r.at[i, k], dev))

    def a2y(i):
        st.yy[i].wait_recv()
        S.ysum[i] = S.ypart[i, half(y), :] + S.yy_r[i].astype(F32)
        plan = ((0, 0, x_f, to_xp), (0, 1, x_f, to_xm), (1, 1, x_p, to_xp), (1, 0, x_m, to_xm))
        for k, s, bx, dev in plan:
            S.yfd_s[i, k, :, side(s)] = S.ysum[i, quarter(bx), side(s)].astype(BF16)
            st.yfd[i, k, s] = go(
                remote(
                    S.yfd_s.at[i, k, :, side_d(s)], S.yfd_r.at[i, k, :, side_d(s)], dev
                )
            )

    def a3x(i):
        for k in (2, 3):
            st.xfd[i, k].wait_recv()
        for k in (0, 1):
            st.xc[i, k].wait_recv()
        for k in (0, 1):
            S.xsum[i, k] = (
                S.xpart[i, block(x, k), :]
                + S.xfd_r[i, 3 - k].astype(F32)
                + S.xc_r[i, k].astype(F32)
            )
        S.xy_s[i] = S.xsum[i, 1 - y].astype(BF16)
        st.xy[i] = go(remote(S.xy_s.at[i], S.xy_r.at[i], to_y))

    def a3y(i):
        for s, bx, dev in ((0, x_p, to_xp), (1, x_m, to_xm)):
            st.yfd[i, 0, s].wait_recv()
            S.yc_s[i, :, side(s)] = (
                S.ysum[i, quarter(bx), side(s)] + S.yfd_r[i, 0, :, side(s)].astype(F32)
            ).astype(BF16)
            st.yc[i, s] = go(
                remote(S.yc_s.at[i, :, side_d(s)], S.yc_r.at[i, :, side_d(s)], dev)
            )

    def activate(i, total, w, grad, cols):
        gate, up, hg = total[:, :w], total[:, w : 2 * w], total[:, 2 * w :]
        sig = jax.nn.sigmoid(gate)
        silu = gate * sig
        mine = block(x, y)
        grad[i, mine, 0:w] = (hg * up * sig * (1.0 + gate * (1.0 - sig))).astype(BF16)
        grad[i, mine, w : 2 * w] = (hg * silu).astype(BF16)
        S.hidden[i * BLK : (i + 1) * BLK, cols] = (silu * up).astype(BF16)

    def a4x(i):
        st.xy[i].wait_recv()
        activate(i, S.xsum[i, y] + S.xy_r[i].astype(F32), XW, S.xgrad, XC)
        slot = S.xgrad.at[i, block(x, y)]
        st.xown_y[i] = go(remote(slot, slot, to_y))
        st.xown_p[i] = go(remote(slot, slot, to_xp))
        st.xown_m[i] = go(remote(slot, slot, to_xm))

    def a4y(i):
        for s in (0, 1):
            st.yfd[i, 1, s].wait_recv()
            st.yc[i, s].wait_recv()
        total = (
            S.ysum[i, quarter(x), :] + S.yfd_r[i, 1].astype(F32) + S.yc_r[i].astype(F32)
        )
        activate(i, total, YW, S.ygrad, YC)
        slot = S.ygrad.at[i, block(x, y)]
        st.yown_p[i] = go(remote(slot, slot, to_xp))
        st.yown_m[i] = go(remote(slot, slot, to_xm))
        st.yown_y[i] = go(remote(slot, slot, to_y))

    def b2x(i):
        st.xown_y[i].wait_recv()
        slot = S.xgrad.at[i, block(x, 1 - y)]
        st.xoth_p[i] = go(remote(slot, slot, to_xp))
        st.xoth_m[i] = go(remote(slot, slot, to_xm))

    def b2y(i):
        left, right = pl.ds(0, YW), pl.ds(YW, YW)
        st.yown_p[i].wait_recv()
        part = S.ygrad.at[i, block(x_m, y), left]
        st.yfar_p[i] = go(remote(part, part, to_xp))
        slot = S.ygrad.at[i, block(x_m, y)]
        st.yy_m[i] = go(remote(slot, slot, to_y))
        st.yown_m[i].wait_recv()
        part = S.ygrad.at[i, block(x_p, y), right]
        st.yfar_m[i] = go(remote(part, part, to_xm))
        slot = S.ygrad.at[i, block(x_p, y)]
        st.yy_p[i] = go(remote(slot, slot, to_y))

    def b3x(i):
        st.xown_p[i].wait_recv()
        slot = S.xgrad.at[i, block(x_m, y)]
        st.xfar_p[i] = go(remote(slot, slot, to_xp))
        st.xoth_m[i].wait_recv()
        slot = S.xgrad.at[i, block(x_p, 1 - y)]
        st.xfar_m[i] = go(remote(slot, slot, to_xm))

    def b3y(i):
        st.yfar_p[i].wait_recv()
        st.yfar_m[i].wait_recv()
        slot = S.ygrad.at[i, block(x_f, y)]
        st.yy_f[i] = go(remote(slot, slot, to_y))

    def owner_core(i):
        return i % 2

    def owner_yh(i):
        return i // 2

    def part_cols(i, q):
        w = FEAT // n_parts(i)
        return slice(q * w, (q + 1) * w), pl.ds(q * w, w)

    def b4x(i):
        for copies in (st.xown_m, st.xoth_p, st.xfar_p, st.xfar_m):
            copies[i].wait_recv()
        S.acc[i] = dot_t(S.xgrad[i], S.wx[...])

    def b4y(i):
        for copies in (st.yown_y, st.yy_m, st.yy_p, st.yy_f):
            copies[i].wait_recv()
        away = core != owner_core(i)
        for q in range(n_parts(i)):
            cols, cols_d = part_cols(i, q)
            S.acc[i, :, cols] += dot_t(S.ygrad[i], S.wy[cols, :])
            st.core[i, q] = remote(S.acc.at[i, :, cols_d], S.core_r.at[i, :, cols_d], to_core)
            pl.when(away)(lambda q=q: go(st.core[i, q], away) and None)

    def z_rows(j):
        return pl.ds(pl.multiple_of(lax.rem(z + j, 8) * BLK, BLK), BLK)

    def c2(i, q=0):
        here = core == owner_core(i)
        cols, cols_d = part_cols(i, q)
        for j in range(1, 8):
            dev = fsdp(lax.rem(f + 4 * j, 32))
            st.z[i, q, j] = remote(S.z_s.at[i, j, :, cols_d], S.z_r.at[i, j, :, cols_d], dev)

        @pl.when(here)
        def _():
            st.core[i, q].wait_recv()
            for j in (4, 3, 5, 2, 6, 1, 7):
                rows = z_rows(j)
                S.z_s[i, j, :, cols] = (
                    S.acc[i, rows, cols] + S.core_r[i, rows, cols]
                ).astype(BF16)
                go(st.z[i, q, j], here)

    def c3(i, q=0):
        here = core == owner_core(i)
        away = jnp.logical_and(here, yh != owner_yh(i))
        cols, cols_d = part_cols(i, q)
        st.yh[i, q] = remote(S.yh_s.at[i, :, cols_d], S.yh_r.at[i, :, cols_d], to_yh)

        @pl.when(here)
        def _():
            rows = z_rows(0)
            total = S.acc[i, rows, cols] + S.core_r[i, rows, cols]
            for j in (1, 7, 2, 6, 3, 5, 4):
                st.z[i, q, j].wait_recv()
                total = total + S.z_r[i, j, :, cols].astype(F32)
            S.yh_s[i, :, cols] = total

        @pl.when(away)
        def _():
            go(st.yh[i, q], away)

    def c4(i, q=0):
        cols, _ = part_cols(i, q)

        @pl.when(jnp.logical_and(core == owner_core(i), yh == owner_yh(i)))
        def _():
            st.yh[i, q].wait_recv()
            gi_o[:, cols] = (S.yh_s[i, :, cols] + S.yh_r[i, :, cols]).astype(BF16)

    def c2_direct(i, q):
        here = core == owner_core(i)
        same = jnp.logical_and(here, yh == owner_yh(i))
        other = jnp.logical_and(here, yh != owner_yh(i))
        cols, cols_d = part_cols(i, q)
        for j in range(8):
            src = S.z_s.at[i, j, :, cols_d]
            dev = lax.rem(f + 4 * j, 32)
            if j:
                st.z[i, q, 0, j] = remote(src, S.z_r.at[i, j, :, cols_d], fsdp(dev))
            dev = fsdp(dev + 2 - 4 * yh)
            st.z[i, q, 1, j] = remote(src, S.other_r.at[i, j, :, cols_d], dev)

        @pl.when(here)
        def _():
            st.core[i, q].wait_recv()

        def send(ring, j, cond):
            rows = z_rows(j)
            S.z_s[i, j, :, cols] = (
                S.acc[i, rows, cols] + S.core_r[i, rows, cols]
            ).astype(BF16)
            go(st.z[i, q, ring, j], cond)

        @pl.when(same)
        def _():
            for j in (4, 3, 5, 2, 6, 1, 7):
                send(0, j, same)

        @pl.when(other)
        def _():
            for j in (4, 3, 5, 2, 6, 1, 7, 0):
                send(1, j, other)

    def c3_direct(i, q):
        cols, _ = part_cols(i, q)

        @pl.when(jnp.logical_and(core == owner_core(i), yh == owner_yh(i)))
        def _():
            rows = z_rows(0)
            total = S.acc[i, rows, cols] + S.core_r[i, rows, cols]
            for j in (1, 7, 0, 2, 6, 3, 5, 4):
                for ring in (0, 1) if j else (1,):
                    st.z[i, q, ring, j].wait_recv()
                    got = S.other_r[i, j, :, cols] if ring else S.z_r[i, j, :, cols]
                    total = total + got.astype(F32)
            gi_o[:, cols] = total.astype(BF16)

    def back_send():
        for b in range(8):
            rows = jnp.concatenate([S.back[i, b] for i in range(BATCHES)], axis=0)
            S.back_s[b] = pack(rows).astype(BF16)
        for j in range(1, 8):
            dst = lax.rem(p + j, 8)
            st.back[j] = go(remote(S.back_s.at[dst], S.back_r.at[j], pipe(dst)))

    def low_1():
        S.low_s[...] = pack(dot_t(S.down_a[...], S.hidden[...]))
        st.low_c[0] = go(remote(S.low_s, S.low_cr, to_core))

    def la_1():
        total = S.back_s[p].astype(F32)
        for j in range(1, 8):
            st.back[j].wait_recv()
            total = total + S.back_r[j].astype(F32)
        back = (0.5 * unpack(total)).astype(BF16)
        S.la_s[...] = dot_lead(back, S.hidden[...])
        for j in range(1, 8):
            dst = lax.rem(p + j, 8)
            rows = S.la_s.at[pl.ds(pl.multiple_of(dst * 8, 8), 8)]
            st.la[j] = go(remote(rows, S.la_r.at[j], pipe(dst)))

    def low_2():
        st.low_c[0].wait_recv()
        rows = pl.ds(pl.multiple_of(core * 16, 16), 16)
        S.low_h[...] = S.low_s[rows, :] + S.low_cr[rows, :]
        for j in range(1, 16):
            dev = fsdp(lax.rem(chip + j, 16) * 2 + core)
            st.low_z[j] = go(remote(S.low_h, S.low_zr.at[j], dev))

    def la_2():
        mine = pl.ds(pl.multiple_of(p * 8, 8), 8)
        total = S.la_s[mine, :]
        for j in range(1, 8):
            st.la[j].wait_recv()
            total = total + S.la_r[j]
        S.la[mine, :] = total
        slot = S.la.at[mine]
        for j in range(1, 8):
            st.la_g[j] = go(remote(slot, slot, pipe(lax.rem(p + j, 8))))

    def low_3():
        total = S.low_h[...]
        for j in range(1, 16):
            st.low_z[j].wait_recv()
            total = total + S.low_zr[j]
        S.low_p[core, p] = total.astype(BF16)
        slot = S.low_p.at[core, p]
        for j in range(1, 8):
            st.low_p[j] = go(remote(slot, slot, pipe(lax.rem(p + j, 8))))

    def low_4():
        for j in range(1, 8):
            st.low_p[j].wait_recv()
        slot = S.low_p.at[core]
        st.low_g[0] = go(remote(slot, slot, to_core))

    def la_3():
        for j in range(1, 8):
            st.la_g[j].wait_recv()
        la_o[...] = S.la[...]

    def low_5():
        st.low_g[0].wait_recv()
        total = None
        for b in range(8):
            v = jnp.concatenate([S.low_p[0, b], S.low_p[1, b]], axis=0).astype(F32)
            low = (0.5 * unpack(v)).astype(BF16)
            v = dot(low, S.cot[:, b].reshape(64, FEAT))
            total = v if total is None else total + v
        lb_o[...] = total

    a1x(0)
    a1y(1)
    a1x(2)
    a1y(0)
    a2x(0)
    a1x(1)
    a1y(2)
    a2x(2)
    a1x(3)
    a3x(0)
    a2y(0)
    a1y(3)
    a2x(1)
    a2y(1)
    a3y(0)
    a4x(0)
    a2x(3)
    a3x(1)
    a3y(1)
    a2y(2)
    a3x(2)
    a4y(0)
    a2y(3)
    b2x(0)
    a3x(3)
    a4x(1)
    b2y(0)
    a3y(3)
    a3y(2)
    a4y(1)
    b3x(0)
    a4x(2)
    b2x(1)
    b3y(0)
    a4x(3)
    a4y(3)
    a4y(2)
    low_1()
    b2y(1)
    b4x(0)
    b2x(2)
    b4y(0)
    b3x(1)
    low_2()
    b2x(3)
    b3y(1)
    back_send()
    b2y(2)
    b2y(3)
    c2(0)
    b3x(2)
    b4x(1)
    b4y(1)
    b3x(3)
    b3y(2)
    la_1()
    b4x(2)
    b3y(3)
    c2(1)
    b4y(2)
    low_3()
    b4x(3)
    la_2()
    c2_direct(2, 0)
    b4y(3)
    c3(0)
    low_4()
    c2_direct(3, 0)
    c2_direct(3, 1)
    low_5()
    la_3()
    c3(1)
    c4(0)
    c3_direct(2, 0)
    c3_direct(3, 0)
    c4(1)
    c3_direct(3, 1)
    for cp, cond in sent:
        if cond is None:
            cp.wait_send()
        else:
            pl.when(cond)(cp.wait_send)


def hand_over(*refs):
    for src, dst in zip(refs[:3], refs[3:]):
        dst[...] = src[...]


def shards(tok, cot, gate_w, up_w, down_w, down_a, down_b):
    any_ = pl.BlockSpec(memory_space=pl.ANY)
    vmem = pl.BlockSpec(memory_space=pltpu.VMEM)
    grad_in, grad_a, grad_b = pl.pallas_call(
        kernel,
        out_shape=(
            jax.ShapeDtypeStruct((16, FEAT), BF16),
            jax.ShapeDtypeStruct((RANK, HID), F32),
            jax.ShapeDtypeStruct((RANK, FEAT), F32),
        ),
        in_specs=[any_] * 7,
        out_specs=(vmem, vmem, vmem),
        scratch_shapes=scratch_spec()[0]
        + [
            pltpu.SemaphoreType.DMA((N_COPIES,)),
            pltpu.SemaphoreType.DMA((N_COPIES,)),
            pltpu.SemaphoreType.DMA((N_LOADS,)),
        ],
        compiler_params=pltpu.CompilerParams(
            collective_id=0, has_side_effects=True, vmem_limit_bytes=60 * 2**20
        ),
    )(tok.reshape(8, 4, BLK, FEAT), cot.reshape(8, 4, BLK, FEAT), gate_w, up_w, down_w, down_a.T, down_b)
    grad_in, grad_a, grad_b = pl.pallas_call(
        hand_over,
        out_shape=(
            jax.ShapeDtypeStruct((16, FEAT), BF16),
            jax.ShapeDtypeStruct((RANK, HID), F32),
            jax.ShapeDtypeStruct((RANK, FEAT), F32),
        ),
        in_specs=[vmem] * 3,
        out_specs=(vmem, vmem, vmem),
    )(grad_in, grad_a, grad_b)
    return grad_in, grad_a.T, grad_b


def solution(mesh):
    return jax.shard_map(
        shards,
        mesh=mesh,
        in_specs=(
            P(None, "pipe"),
            P(None, "pipe"),
            P("pipe", "fsdp"),
            P("pipe", "fsdp"),
            P("fsdp", "pipe"),
            P("fsdp", None),
            P(None, "pipe"),
        ),
        out_specs=(P("fsdp", "pipe"), P("fsdp", None), P(None, "pipe")),
        check_vma=False,
    )
```
